256 devices in a mesh: rows: 16 (over z_hi, y, core), tp: 16 (over x, z_lo).
Axes of the slice: x: 4, y: 4, z: 8 (z_hi: 2, z_lo: 4; z = z_hi * 4 + z_lo), core: 2. Of those that a mesh axis runs over, the one named last changes fastest.
Arguments:
- teacher_hidden: bfloat16 [12288, 8192], P('rows', 'tp'), may hold values from -8 to 8
- norm_gain: float32 [8192], replicated, may hold values from 0.25 to 1.75
- head_weight: bfloat16 [8192, 16384], P('rows', 'tp'), may hold values from -0.19997864 to 0.19997864
- student_logits: bfloat16 [12288, 16384], P('rows', 'tp'), may hold values from -300 to 300
- row_lengths: int32 [3072], P('rows'), may hold values from 1 to 4
Outputs:
- logit_grad: bfloat16 [12288, 16384], P('rows', 'tp')
- loss: float32 [], replicated
The draws below stay inside these ranges and needn't reach their ends.
All inputs are finite; a program needn't handle non-finite values.
Results may differ from the reference program's by a relative error of at most 0.0049.
Values may be sent and summed in bfloat16 or wider, within the bound.
No kernel may reach another device: no remote copies, remote signals or barrier semaphores. Data moves between devices by JAX's collectives and lax.ppermute only.
A program may use at most 128 MiB of HBM per device.

```python
import jax
import jax.numpy as jnp
from jax import lax

D = 8192
V = 2048
CB = 8
STEPS = 4
ROWS = 3072
TOKENS = 12288
VOC = 16384
N_ROWS = 16


def head_base(key, columns):
    base = jax.random.fold_in(key, 11)

    def one_column(column):
        return jax.random.truncated_normal(jax.random.fold_in(base, column), -6.0, 6.0, (D,), jnp.float32)
    return jax.vmap(one_column)(columns)


def draw_head_weight(key, part):
    columns = head_base(key, jnp.arange(VOC, dtype=jnp.int32))
    return (columns.T * (3.0 * D ** (-0.5))).astype(jnp.bfloat16)


def draw_teacher_hidden(key, part):
    own_key = jax.random.fold_in(key, 5)
    values = jax.random.truncated_normal(own_key, -6.0, 6.0, (TOKENS, D), jnp.float32)
    return values.astype(jnp.bfloat16)


def draw_student_logits(key, part):
    key = jax.random.fold_in(key, 7)
    key_base = jax.random.fold_in(key, 0)
    group = jnp.arange(TOKENS, dtype=jnp.int32) * N_ROWS // TOKENS
    ramp = (group.astype(jnp.float32) / max(N_ROWS - 1, 1))[:, None]
    values = (1.5 + 3.0 * ramp) * jax.random.normal(key_base, (TOKENS, VOC), jnp.float32)
    values = jnp.clip(values, -27.0, 27.0)
    return values.astype(jnp.bfloat16)


def draw_row_lengths(key, part):
    key = jax.random.fold_in(key, 13)
    index = jnp.arange(ROWS, dtype=jnp.int32)
    group = index * N_ROWS // ROWS
    level = group * (STEPS - 1) * 2 // max(N_ROWS - 1, 1)
    pick = jax.random.randint(key, (ROWS,), 0, 1 << 20)
    extra = jnp.minimum(pick % (level + 1), STEPS - 1)
    lengths = 1 + extra
    return jnp.where(index == ROWS - 1, STEPS, lengths).astype(jnp.int32)


def setup_inputs(seed: int = 0) -> dict:
    seeds = jax.random.split(jax.random.key(seed), 6)
    return {
        "teacher_hidden": draw_teacher_hidden(jax.random.fold_in(seeds[5], 71), 0),
        "norm_gain": jnp.clip(1.0 + 0.15 * jax.random.normal(seeds[1], (D,), jnp.float32), 0.25, 1.75),
        "head_weight": draw_head_weight(jax.random.fold_in(seeds[5], 71), 0),
        "student_logits": draw_student_logits(jax.random.fold_in(seeds[5], 71), 0),
        "row_lengths": draw_row_lengths(jax.random.fold_in(seeds[5], 71), 0),
    }


def reference(teacher_hidden, norm_gain, head_weight, student_logits, row_lengths):
    group_rows = ROWS // N_ROWS
    group_tok = group_rows * STEPS
    hidden_groups = teacher_hidden.reshape(N_ROWS, group_tok, D)
    student_groups = student_logits.reshape(N_ROWS, group_tok, VOC)
    length_groups = row_lengths.reshape(N_ROWS, group_rows)

    def one_group(items):
        hidden, student, lengths = items
        wide = hidden.astype(jnp.float32)
        scale = lax.rsqrt(lax.optimization_barrier(jnp.mean(wide * wide, axis=-1)) + 1e-05)
        normed = (wide * norm_gain[None, :]).astype(jnp.bfloat16)
        teacher = jnp.dot(normed, head_weight, preferred_element_type=jnp.float32) * scale[:, None]
        teacher_logp = jax.nn.log_softmax(teacher.reshape(group_tok, CB, V), axis=-1)
        student_logp = jax.nn.log_softmax(student.astype(jnp.float32).reshape(group_tok, CB, V), axis=-1)
        prob = jnp.exp(student_logp)
        differ = student_logp - teacher_logp
        divergence = lax.optimization_barrier(jnp.sum(prob * differ, axis=-1))
        steps_of = jnp.arange(group_tok, dtype=jnp.int32) % STEPS
        live = (steps_of < jnp.repeat(lengths, STEPS)).astype(jnp.float32)
        grad = V * live[:, None, None] * prob * (differ - divergence[:, :, None])
        grad = grad.reshape(group_tok, VOC).astype(jnp.bfloat16)
        return (grad, jnp.sum(live[:, None] * divergence))
    grads, partial_value = lax.map(one_group, (hidden_groups, student_groups, length_groups))
    total_len = jnp.sum(row_lengths.astype(jnp.float32))
    loss = jnp.sum(partial_value) / (CB * total_len)
    return (grads.reshape(TOKENS, VOC), loss)
```

```python
import jax
import jax.numpy as jnp
from jax import lax
from jax.experimental import pallas as pl
from jax.experimental.pallas import tpu as pltpu
from jax.sharding import PartitionSpec as P

V = 2048
CB = 8
STEPS = 4
NX = 4
NZ = 4
NY = 4
NH = 2
BLOCKS = 16
CHUNK = 128
MIB = 1 << 20


def tp_at(x, z):
    return x * NZ + z


def row_at(h, y, c):
    return h * 2 * NY + y * 2 + c


def x_ring(d):
    return [(tp_at(x, z), tp_at((x + d) % NX, z)) for x in range(NX) for z in range(NZ)]


def z_ring(d):
    return [(tp_at(x, z), tp_at(x, (z + d) % NZ)) for x in range(NX) for z in range(NZ)]


def y_ring(d):
    return [
        (row_at(h, y, c), row_at(h, (y + d) % NY, c))
        for h in range(NH)
        for y in range(NY)
        for c in range(2)
    ]


def row_xor(m):
    return [(r, r ^ m) for r in range(16)]


PAIR = [(t, t ^ 1) for t in range(16)]
SAME_HALF = [[row_at(h, y, c) for y in range(NY) for c in range(2)] for h in range(NH)]


def after(value, *earlier):
    return lax.optimization_barrier((value,) + earlier)[0]


def gather_hidden(own):
    half = own.shape[0] // 2
    blocks = []
    held = own
    gate = ()
    for i in range(NZ):
        nxt = lax.ppermute(held, "tp", z_ring(1)) if i < NZ - 1 else None
        ready = after(held, *gate) if gate else held
        left = lax.ppermute(ready, "tp", x_ring(1))
        right = lax.ppermute(ready, "tp", x_ring(-1))
        top = lax.ppermute(left[:half], "tp", x_ring(1))
        low = lax.ppermute(right[half:], "tp", x_ring(-1))
        blocks += [held, left, right, top, low]
        gate = (left, right)
        held = nxt
    return blocks


def teacher_kernel(slots_ref, gain_ref, student_ref, *refs):
    a_refs, (w_own, w_far) = refs[:20], refs[20:22]
    teach_ref, stats_ref = refs[22:24]
    a_vm, w_vm, square_ref, a_sem, w_sem = refs[24:]
    tok = teach_ref.shape[0]
    half = tok // 2

    for step in range(BLOCKS):
        group = a_refs[5 * (step // 4) : 5 * (step // 4) + 5]
        j = step % 4
        if j < 3:
            pltpu.make_async_copy(group[j], a_vm.at[step], a_sem.at[step]).start()
        else:
            pltpu.make_async_copy(
                group[3], a_vm.at[step, pl.ds(0, half)], a_sem.at[step]
            ).start()
            pltpu.make_async_copy(
                group[4], a_vm.at[step, pl.ds(half, half)], a_sem.at[step]
            ).start()
        slot = slots_ref[step]

        @pl.when(slot < 8)
        def _():
            pltpu.make_async_copy(w_own.at[slot], w_vm.at[step], w_sem.at[step]).start()

        @pl.when(slot >= 8)
        def _():
            pltpu.make_async_copy(w_far.at[slot - 8], w_vm.at[step], w_sem.at[step]).start()

    square_ref[...] = jnp.zeros_like(square_ref)
    teach_ref[...] = jnp.zeros_like(teach_ref)

    def step_body(step, carry):
        pltpu.make_async_copy(a_vm.at[step], a_vm.at[step], a_sem.at[step]).wait()
        pltpu.make_async_copy(w_vm.at[step], w_vm.at[step], w_sem.at[step]).wait()
        gain = gain_ref[slots_ref[BLOCKS + step]]
        for r in range(0, tok, 256):
            wide = a_vm[step, r : r + 256, :].astype(jnp.float32)
            square = wide * wide
            square_ref[r : r + 256, :] += (
                square[:, :128] + square[:, 128:256] + square[:, 256:384] + square[:, 384:]
            )
            normed = (wide * gain).astype(jnp.bfloat16)
            teach_ref[r : r + 256, :] += jnp.dot(
                normed, w_vm[step], preferred_element_type=jnp.float32
            )
        return carry

    lax.fori_loop(0, BLOCKS, step_body, 0)

    lane = lax.broadcasted_iota(jnp.int32, (CHUNK, 128), 1)
    for r in range(0, tok, CHUNK):
        rows = pl.ds(r, CHUNK)
        mean = jnp.sum(square_ref[rows, :], axis=1, keepdims=True) / (BLOCKS * 512)
        teach = teach_ref[rows, :] * lax.rsqrt(mean + 1e-05)
        teach_ref[rows, :] = teach
        stud = student_ref[rows, :].astype(jnp.float32)
        teach_peak = jnp.max(teach, axis=1, keepdims=True)
        stud_peak = jnp.max(stud, axis=1, keepdims=True)
        teach = teach - teach_peak
        stud = stud - stud_peak
        mass = jnp.exp(stud)
        teach_total = jnp.sum(jnp.exp(teach), axis=1, keepdims=True)
        stud_total = jnp.sum(mass, axis=1, keepdims=True)
        cross = jnp.sum(mass * (stud - teach), axis=1, keepdims=True)
        packed = jnp.zeros((CHUNK, 128), jnp.float32)
        for at, value in enumerate((teach_peak, teach_total, stud_peak, stud_total, cross)):
            packed = jnp.where(lane == at, value, packed)
        stats_ref[:, r : r + CHUNK] = packed.T[:8, :]


def teacher_logits(hidden, near, far, gain, student, slots):
    tok, cols = student.shape
    any_space = pl.BlockSpec(memory_space=pl.ANY)
    vmem = pl.BlockSpec(memory_space=pltpu.VMEM)
    return pl.pallas_call(
        teacher_kernel,
        out_shape=(
            jax.ShapeDtypeStruct((tok, cols), jnp.float32),
            jax.ShapeDtypeStruct((8, tok), jnp.float32),
        ),
        in_specs=[pl.BlockSpec(memory_space=pltpu.SMEM), vmem, vmem] + [any_space] * 22,
        out_specs=(vmem, vmem),
        scratch_shapes=[
            pltpu.VMEM((BLOCKS, tok, 512), jnp.bfloat16),
            pltpu.VMEM((BLOCKS, 512, cols), jnp.bfloat16),
            pltpu.VMEM((tok, 128), jnp.float32),
            pltpu.SemaphoreType.DMA((BLOCKS,)),
            pltpu.SemaphoreType.DMA((BLOCKS,)),
        ],
        compiler_params=pltpu.CompilerParams(vmem_limit_bytes=52 * MIB),
        name="teacher",
    )(slots, gain.reshape(BLOCKS, 1, 512), student, *hidden, near, far)


def grad_kernel(coef_ref, teach_ref, student_ref, grad_ref):
    coef = coef_ref[...].T
    stud = student_ref[...].astype(jnp.float32)
    prob = jnp.exp((stud - coef[:, 0:1]) - coef[:, 1:2])
    differ = (stud - teach_ref[...]) - coef[:, 2:3]
    grad_ref[...] = ((coef[:, 3:4] * prob) * differ).astype(jnp.bfloat16)


def gradient(coef, teach, student):
    tok, cols = student.shape
    tile = 256
    return pl.pallas_call(
        grad_kernel,
        grid=(tok // tile,),
        out_shape=jax.ShapeDtypeStruct((tok, cols), jnp.bfloat16),
        in_specs=[
            pl.BlockSpec((8, tile), lambda i: (0, i)),
            pl.BlockSpec((tile, cols), lambda i: (i, 0)),
            pl.BlockSpec((tile, cols), lambda i: (i, 0)),
        ],
        out_specs=pl.BlockSpec((tile, cols), lambda i: (i, 0)),
        compiler_params=pltpu.CompilerParams(vmem_limit_bytes=32 * MIB),
        name="gradient",
    )(coef, teach, student)


def total_everywhere(value):
    for axis, moves in (
        ("rows", [row_xor(m) for m in (1, 8, 9)]),
        ("tp", [z_ring(d) for d in (1, 2, 3)]),
        ("rows", [y_ring(d) for d in (1, 2, 3)]),
        ("tp", [x_ring(d) for d in (1, 2, 3)]),
    ):
        first, second, third = [lax.ppermute(value, axis, m) for m in moves]
        value = (value + first) + (second + third)
    return value


def body(teacher_hidden, norm_gain, head_weight, student_logits, row_lengths):
    tok = teacher_hidden.shape[0]
    far_shard = lax.ppermute(head_weight, "rows", row_xor(8))
    near = lax.all_gather(head_weight, "rows", axis_index_groups=SAME_HALF)
    far = lax.all_gather(far_shard, "rows", axis_index_groups=SAME_HALF)
    hidden = gather_hidden(teacher_hidden)

    tp = lax.axis_index("tp")
    half = lax.axis_index("rows") // 8
    z_off = jnp.arange(BLOCKS, dtype=jnp.int32) // 4
    x_off = jnp.asarray([0, 1, 3, 2] * 4, jnp.int32)
    block = ((tp // NZ - x_off) % NX) * NZ + (tp % NZ - z_off) % NZ
    slot = jnp.where(block // 8 == half, block % 8, 8 + block % 8)
    slots = jnp.concatenate([slot, block]).astype(jnp.int32)
    teach, stats = teacher_logits(hidden, near, far, norm_gain, student_logits, slots)

    other = lax.ppermute(stats, "tp", PAIR)
    teach_peak = jnp.maximum(stats[0], other[0])
    stud_peak = jnp.maximum(stats[2], other[2])
    teach_total = stud_total = cross = 0.0
    for part in (stats, other):
        teach_low = part[0] - teach_peak
        stud_low = part[2] - stud_peak
        weight = jnp.exp(stud_low)
        teach_total = teach_total + jnp.exp(teach_low) * part[1]
        stud_total = stud_total + weight * part[3]
        cross = cross + weight * (part[4] + part[3] * (stud_low - teach_low))
    log_stud = jnp.log(stud_total)
    log_teach = jnp.log(teach_total)
    divergence = cross / stud_total - (log_stud - log_teach)
    steps_of = jnp.arange(tok, dtype=jnp.int32) % STEPS
    live = (steps_of < jnp.repeat(row_lengths, STEPS)).astype(jnp.float32)
    offset = (stud_peak - teach_peak) + (log_stud - log_teach) + divergence
    none = jnp.zeros_like(live)
    coef = jnp.stack([stud_peak, log_stud, offset, V * live, none, none, none, none])
    grad = gradient(coef, teach, student_logits)

    sums = jnp.stack([jnp.sum(live * divergence), jnp.sum(row_lengths.astype(jnp.float32))])
    sums = total_everywhere(sums.reshape(1, 2))
    loss = (0.5 * sums[0, 0]) / (CB * (sums[0, 1] / BLOCKS))
    return (grad, loss)


def solution(mesh):
    in_specs = (P("rows", "tp"), P(), P("rows", "tp"), P("rows", "tp"), P("rows"))
    out_specs = (P("rows", "tp"), P())
    return jax.shard_map(body, mesh=mesh, in_specs=in_specs, out_specs=out_specs, check_vma=False)
```

```python
import functools

import jax
import jax.numpy as jnp
from jax import lax
from jax.experimental import pallas as pl
from jax.experimental.pallas import tpu as pltpu
from jax.sharding import PartitionSpec as P

V = 2048
CB = 8
STEPS = 4
NX = 4
NZ = 4
NY = 4
NH = 2
BLOCKS = 16
CHUNK = 128
MIB = 1 << 20


def tp_at(x, z):
    return x * NZ + z


def row_at(h, y, c):
    return h * 2 * NY + y * 2 + c


def x_ring(d):
    return [(tp_at(x, z), tp_at((x + d) % NX, z)) for x in range(NX) for z in range(NZ)]


def z_ring(d):
    return [(tp_at(x, z), tp_at(x, (z + d) % NZ)) for x in range(NX) for z in range(NZ)]


def y_ring(d):
    return [
        (row_at(h, y, c), row_at(h, (y + d) % NY, c))
        for h in range(NH)
        for y in range(NY)
        for c in range(2)
    ]


def z_whole(d):
    at = [(h, z) for h in range(NH) for z in range(NZ)]
    moves = [(one, at[(i + d) % len(at)]) for i, one in enumerate(at)]
    return [
        (row_at(h, y, c) * BLOCKS + tp_at(x, z), row_at(h2, y, c) * BLOCKS + tp_at(x, z2))
        for (h, z), (h2, z2) in moves
        for y in range(NY)
        for c in range(2)
        for x in range(NX)
    ]


def row_xor(m):
    return [(r, r ^ m) for r in range(16)]


PAIR = [(t, t ^ 1) for t in range(16)]
SAME_HALF = [[row_at(h, y, c) for y in range(NY) for c in range(2)] for h in range(NH)]


def after(value, *earlier):
    return lax.optimization_barrier((value,) + earlier)[0]


def teacher_logits(weight, own, accumulate):
    half = own.shape[0] // 2
    cut = weight.shape[0] // 2

    def x_hop(value, d):
        return lax.ppermute(value, "tp", x_ring(d))

    def z_hop(value):
        return lax.ppermute(value, "tp", z_ring(1))

    def widen(shard):
        return lax.all_gather(shard, "rows", axis_index_groups=SAME_HALF)

    def far_hop(value, d):
        return lax.ppermute(value, ("rows", "tp"), z_whole(d))

    near = widen(weight)
    z1 = z_hop(own)
    left0, right0 = x_hop(own, 1), x_hop(own, -1)
    up, down = far_hop(weight[:cut], 2), far_hop(weight[cut:], -2)
    top0, low0 = x_hop(left0[:half], 1), x_hop(right0[half:], -1)

    here1, up, down, *_ = lax.optimization_barrier((z1, up, down, top0, low0))
    left1, right1 = x_hop(here1, 1), x_hop(here1, -1)
    up, down = far_hop(up, 2), far_hop(down, -2)
    up, down, here1, to_right, to_left = lax.optimization_barrier(
        (up, down, here1, left1, right1)
    )
    far = widen(jnp.concatenate([up, down]))
    z2 = z_hop(here1)
    top1, low1 = x_hop(to_right[:half], 1), x_hop(to_left[half:], -1)

    here2, *_ = lax.optimization_barrier((z2, top1, low1))
    z3 = z_hop(here2)
    left2, right2 = x_hop(here2, 1), x_hop(here2, -1)

    here3, to_right, to_left = lax.optimization_barrier((z3, left2, right2))
    left3, right3 = x_hop(here3, 1), x_hop(here3, -1)
    top2, low2 = x_hop(to_right[:half], 1), x_hop(to_left[half:], -1)
    blocks = [(own,), (left0,), (top0, low0), (right0,)]
    blocks += [(z1,), (left1,), (top1, low1), (right1,)]
    state = accumulate(0, blocks, near, far)

    to_right, to_left, *_ = lax.optimization_barrier((left3, right3, top2, low2, *state))
    top3, low3 = x_hop(to_right[:half], 1), x_hop(to_left[half:], -1)
    blocks = [(z2,), (left2,), (top2, low2), (right2,), (z3,), (left3,), (right3,)]
    state = accumulate(8, blocks, near, far, state)
    return accumulate(15, [(top3, low3)], near, far, state)


def start_block(block, to, sem):
    at = 0
    for part in block:
        rows = part.shape[0]
        pltpu.make_async_copy(part, to.at[pl.ds(at, rows)], sem).start()
        at += rows


def teacher_kernel(first, shape, plan_ref, gain_ref, near_ref, far_ref, *refs):
    refs = list(refs)
    count = len(shape)
    last = first + count == BLOCKS
    student_ref = refs.pop(0) if last else None
    start_refs = [refs.pop(0), refs.pop(0)] if first else []
    blocks = [[refs.pop(0) for _ in range(parts)] for parts in shape]
    teach_ref, side_ref, a_vm, w_vm, a_sem, w_sem, start_sem, *square_ref = refs
    square_ref = square_ref[0] if last else side_ref
    tok = teach_ref.shape[0]
    starts = [
        pltpu.make_async_copy(ref, to, start_sem.at[at])
        for at, (ref, to) in enumerate(zip(start_refs, (teach_ref, square_ref)))
    ]
    for step in range(count):
        start_block(blocks[step], a_vm.at[step], a_sem.at[step])
        slot = plan_ref[first + step]

        @pl.when(slot < 8)
        def _():
            pltpu.make_async_copy(near_ref.at[slot], w_vm.at[step], w_sem.at[step]).start()

        @pl.when(slot >= 8)
        def _():
            pltpu.make_async_copy(far_ref.at[slot - 8], w_vm.at[step], w_sem.at[step]).start()

        if step == 0:
            for copy in starts:
                copy.start()
    if first:
        for copy in starts:
            copy.wait()
    else:
        square_ref[...] = jnp.zeros_like(square_ref)
        teach_ref[...] = jnp.zeros_like(teach_ref)

    def step_body(step, carry):
        pltpu.make_async_copy(a_vm.at[step], a_vm.at[step], a_sem.at[step]).wait()
        pltpu.make_async_copy(w_vm.at[step], w_vm.at[step], w_sem.at[step]).wait()
        gain = gain_ref[plan_ref[BLOCKS + first + step]]
        for r in range(0, tok, 256):
            wide = a_vm[step, r : r + 256, :].astype(jnp.float32)
            square = wide * wide
            square_ref[r : r + 256, :] += (
                square[:, :128] + square[:, 128:256] + square[:, 256:384] + square[:, 384:]
            )
            normed = (wide * gain).astype(jnp.bfloat16)
            teach_ref[r : r + 256, :] += jnp.dot(
                normed, w_vm[step], preferred_element_type=jnp.float32
            )
        return carry

    lax.fori_loop(0, count, step_body, 0)
    if last:
        statistics(teach_ref, square_ref, student_ref, side_ref)


def statistics(teach_ref, square_ref, student_ref, stats_ref):
    lane = lax.broadcasted_iota(jnp.int32, (CHUNK, 128), 1)
    for r in range(0, teach_ref.shape[0], CHUNK):
        rows = pl.ds(r, CHUNK)
        mean = jnp.sum(square_ref[rows, :], axis=1, keepdims=True) / (BLOCKS * 512)
        teach = teach_ref[rows, :] * lax.rsqrt(mean + 1e-05)
        teach_ref[rows, :] = teach
        stud = student_ref[rows, :].astype(jnp.float32)
        teach_peak = jnp.max(teach, axis=1, keepdims=True)
        stud_peak = jnp.max(stud, axis=1, keepdims=True)
        teach = teach - teach_peak
        stud = stud - stud_peak
        mass = jnp.exp(stud)
        teach_total = jnp.sum(jnp.exp(teach), axis=1, keepdims=True)
        stud_total = jnp.sum(mass, axis=1, keepdims=True)
        cross = jnp.sum(mass * (stud - teach), axis=1, keepdims=True)
        packed = jnp.zeros((CHUNK, 128), jnp.float32)
        for at, value in enumerate((teach_peak, teach_total, stud_peak, stud_total, cross)):
            packed = jnp.where(lane == at, value, packed)
        stats_ref[:, r : r + CHUNK] = packed.T[:8, :]


def accumulate_blocks(gain, student, plan, first, blocks, near, far, state=()):
    tok, cols = student.shape
    hbm = pl.BlockSpec(memory_space=pltpu.HBM)
    vmem = pl.BlockSpec(memory_space=pltpu.VMEM)
    smem = pl.BlockSpec(memory_space=pltpu.SMEM)
    logits = jax.ShapeDtypeStruct((tok, cols), jnp.float32)
    squares = jax.ShapeDtypeStruct((tok, 128), jnp.float32)
    stats = jax.ShapeDtypeStruct((8, tok), jnp.float32)
    count = len(blocks)
    last = first + count == BLOCKS
    parts = [part for block in blocks for part in block]
    scratch = [
        pltpu.VMEM((count, tok, 512), jnp.bfloat16),
        pltpu.VMEM((count, 512, cols), jnp.bfloat16),
        pltpu.SemaphoreType.DMA((count,)),
        pltpu.SemaphoreType.DMA((count,)),
        pltpu.SemaphoreType.DMA((2,)),
    ]
    return pl.pallas_call(
        functools.partial(teacher_kernel, first, [len(block) for block in blocks]),
        out_shape=(logits, stats if last else squares),
        in_specs=[smem, vmem, hbm, hbm] + [vmem] * last + [hbm] * (len(state) + len(parts)),
        out_specs=(vmem, vmem),
        scratch_shapes=scratch + [pltpu.VMEM((tok, 128), jnp.float32)] * last,
        compiler_params=pltpu.CompilerParams(vmem_limit_bytes=60 * MIB),
        name="teacher_" + str(first),
    )(plan, gain.reshape(BLOCKS, 1, 512), near, far, *([student] * last), *state, *parts)


def block_plan():
    tp = lax.axis_index("tp")
    half = lax.axis_index("rows") // 8
    x, z = tp // NZ, tp % NZ
    blocks = []
    for i in range(NZ):
        for off in (0, 1, 2, 3) if i < 3 else (0, 1, 3, 2):
            blocks.append(((x - off) % NX) * NZ + (z - i) % NZ)
    slots = [jnp.where(k // 8 == half, k % 8, 8 + k % 8) for k in blocks]
    return jnp.stack(slots + blocks).astype(jnp.int32)


def combine_kernel(own_ref, other_ref, live_ref, count_ref, coef_ref, sums_ref):
    own = [own_ref[at : at + 1, :] for at in range(5)]
    other = [other_ref[at : at + 1, :] for at in range(5)]
    live = live_ref[...]
    teach_peak = jnp.maximum(own[0], other[0])
    stud_peak = jnp.maximum(own[2], other[2])
    teach_total = stud_total = cross = 0.0
    for part in (own, other):
        teach_low = part[0] - teach_peak
        stud_low = part[2] - stud_peak
        weight = jnp.exp(stud_low)
        teach_total = teach_total + jnp.exp(teach_low) * part[1]
        stud_total = stud_total + weight * part[3]
        cross = cross + weight * (part[4] + part[3] * (stud_low - teach_low))
    log_stud = jnp.log(stud_total)
    log_teach = jnp.log(teach_total)
    divergence = cross / stud_total - (log_stud - log_teach)
    coef_ref[...] = jnp.zeros_like(coef_ref)
    coef_ref[0:1, :] = stud_peak
    coef_ref[1:2, :] = log_stud
    coef_ref[2:3, :] = (stud_peak - teach_peak) + (log_stud - log_teach) + divergence
    coef_ref[3:4, :] = V * live
    lane = lax.broadcasted_iota(jnp.int32, (1, 128), 1)
    total = jnp.sum(live * divergence, axis=1, keepdims=True)
    sums_ref[...] = jnp.where(lane == 0, total, jnp.where(lane == 1, count_ref[0], 0.0))


def combine(own, other, live, count):
    vmem = pl.BlockSpec(memory_space=pltpu.VMEM)
    return pl.pallas_call(
        combine_kernel,
        out_shape=(
            jax.ShapeDtypeStruct(own.shape, jnp.float32),
            jax.ShapeDtypeStruct((1, 128), jnp.float32),
        ),
        in_specs=[vmem, vmem, vmem, pl.BlockSpec(memory_space=pltpu.SMEM)],
        out_specs=(vmem, vmem),
        name="combine",
    )(own, other, live, count)


def grad_kernel(coef_ref, teach_ref, student_ref, grad_ref):
    coef = coef_ref[...].T
    stud = student_ref[...].astype(jnp.float32)
    prob = jnp.exp((stud - coef[:, 0:1]) - coef[:, 1:2])
    differ = (stud - teach_ref[...]) - coef[:, 2:3]
    grad_ref[...] = ((coef[:, 3:4] * prob) * differ).astype(jnp.bfloat16)


def gradient(coef, teach, student):
    tok, cols = student.shape
    tile = 256
    return pl.pallas_call(
        grad_kernel,
        grid=(tok // tile,),
        out_shape=jax.ShapeDtypeStruct((tok, cols), jnp.bfloat16),
        in_specs=[
            pl.BlockSpec((8, tile), lambda i: (0, i)),
            pl.BlockSpec((tile, cols), lambda i: (i, 0)),
            pl.BlockSpec((tile, cols), lambda i: (i, 0)),
        ],
        out_specs=pl.BlockSpec((tile, cols), lambda i: (i, 0)),
        compiler_params=pltpu.CompilerParams(vmem_limit_bytes=60 * MIB),
        name="gradient",
    )(coef, teach, student)


def total_everywhere(value):
    for axis, moves in (
        ("tp", [[(t, t ^ 2) for t in range(BLOCKS)]]),
        ("rows", [row_xor(m) for m in (1, 8, 9)]),
        ("rows", [y_ring(d) for d in (1, 2, 3)]),
        ("tp", [x_ring(d) for d in (1, 2, 3)]),
    ):
        value = sum([lax.ppermute(value, axis, move) for move in moves], value)
    return value


def body(teacher_hidden, norm_gain, head_weight, student_logits, row_lengths):
    tok = teacher_hidden.shape[0]
    steps_of = jnp.arange(tok, dtype=jnp.int32) % STEPS
    live = (steps_of < jnp.repeat(row_lengths, STEPS)).astype(jnp.float32)
    count = jnp.sum(row_lengths.astype(jnp.float32))
    accumulate = functools.partial(accumulate_blocks, norm_gain, student_logits, block_plan())
    teach, stats = teacher_logits(head_weight, teacher_hidden, accumulate)
    other = lax.ppermute(stats, "tp", PAIR)
    coef, sums = combine(stats, other, live.reshape(1, tok), count.reshape(1))
    grad = gradient(coef, teach, student_logits)
    sums = total_everywhere(sums)
    loss = sums[0, 0] / (CB * (sums[0, 1] / (BLOCKS // 2)))
    return (grad, loss)


def solution(mesh):
    in_specs = (P("rows", "tp"), P(), P("rows", "tp"), P("rows", "tp"), P("rows"))
    out_specs = (P("rows", "tp"), P())
    return jax.shard_map(body, mesh=mesh, in_specs=in_specs, out_specs=out_specs, check_vma=False)
```

```python
import functools
import itertools

import jax
import jax.numpy as jnp
from jax import lax
from jax.experimental import pallas as pl
from jax.experimental.pallas import tpu as pltpu
from jax.sharding import PartitionSpec as P

V = 2048
CB = 8
STEPS = 4
NX = 4
NZ = 4
NY = 4
NH = 2
BLOCKS = 16
CHUNK = 128
MIB = 1 << 20


def tp_at(x, z):
    return x * NZ + z


def row_at(h, y, c):
    return h * 2 * NY + y * 2 + c


def x_ring(d):
    return [(tp_at(x, z), tp_at((x + d) % NX, z)) for x in range(NX) for z in range(NZ)]


def z_ring(d):
    return [(tp_at(x, z), tp_at(x, (z + d) % NZ)) for x in range(NX) for z in range(NZ)]


def y_ring(d):
    return [
        (row_at(h, y, c), row_at(h, (y + d) % NY, c))
        for h in range(NH)
        for y in range(NY)
        for c in range(2)
    ]


def whole(move):
    places = itertools.product(range(NH), range(NY), range(2), range(NX), range(NZ))

    def at(h, y, c, x, z):
        return row_at(h, y, c) * BLOCKS + tp_at(x, z)

    return [(at(*place), at(*move(*place))) for place in places]


def way(c):
    return 1 - 2 * c


def x_first(h, y, c, x, z):
    return h, y, c, (x + way(c)) % NX, z


def x_second(h, y, c, x, z):
    return h, y, c, (x - way(c)) % NX, z


def z_two(h, y, c, x, z):
    there = (h * NZ + z + 2 * way(c)) % (NH * NZ)
    return there // NZ, y, c, x, there % NZ


def row_xor(m):
    return [(r, r ^ m) for r in range(16)]


SAME_HALF = [[row_at(h, y, c) for y in range(NY) for c in range(2)] for h in range(NH)]


def teacher_logits(weight, own, accumulate):
    def first(value):
        return lax.ppermute(value, ("rows", "tp"), whole(x_first))

    def second(value):
        return lax.ppermute(value, ("rows", "tp"), whole(x_second))

    def far_hop(value):
        return lax.ppermute(value, ("rows", "tp"), whole(z_two))

    def z_hop(value, d):
        return lax.ppermute(value, "tp", z_ring(d))

    def widen(shard):
        return lax.all_gather(shard, "rows", axis_index_groups=SAME_HALF)

    near = widen(weight)
    z1 = z_hop(own, 1)
    half_way = far_hop(weight)
    first0, second0 = first(own), second(own)
    third0 = first(first0)

    here1, half_way, own, *_ = lax.optimization_barrier((z1, half_way, own, second0, third0))
    first1, second1 = first(here1), second(here1)
    third1 = first(first1)
    far = far_hop(half_way)
    z3 = z_hop(own, -1)

    far, here3, here1, *_ = lax.optimization_barrier((far, z3, here1, second1, third1))
    far = widen(far)
    z2 = z_hop(here1, 1)
    first3, second3 = first(here3), second(here3)
    groups = [[own, first0, third0, second0], [here1, first1, third1, second1]]
    state = accumulate(0, [groups[0], groups[0], groups[1], groups[1]], near, near)

    here2, on3, *_ = lax.optimization_barrier((z2, second3, first3, state))
    first2, third3 = first(here2), second(on3)

    here2, on2, *_ = lax.optimization_barrier((here2, first2, third3))
    second2, third2 = second(here2), first(on2)
    blocks = [groups[0], groups[0], groups[1], groups[1]]
    blocks += [[one] for one in (here3, first3, second3, third3, here2, first2)]
    state = accumulate(4, blocks, near, far, state)
    return accumulate(14, [[second2], [third2]], near, far, state)


ORDER = [(0, None), (0, None), (1, None), (1, None)] * 2
ORDER += [(3, 0), (3, 1), (3, 3), (3, 2), (2, 0), (2, 1), (2, 3), (2, 2)]


def block_plan():
    tp = lax.axis_index("tp")
    row = lax.axis_index("rows")
    half = row // 8
    turn = way(row % 2)
    x, z = tp // NZ, tp % NZ
    offsets, blocks, slots = [], [], []
    for step, (i, off) in enumerate(ORDER):
        if off is None:
            side = half if step < 4 else 1 - half
            off = ((x - (2 * side + step % 2)) * turn) % NX
        block = ((x - off * turn) % NX) * NZ + (z - i) % NZ
        offsets.append(jnp.asarray(off, jnp.int32))
        blocks.append(block)
        slots.append(jnp.where(block // 8 == half, block % 8, 8 + block % 8))
    return jnp.stack(slots + blocks + offsets).astype(jnp.int32)


def teacher_kernel(first, choices, plan_ref, gain_ref, near_ref, far_ref, *refs):
    refs = list(refs)
    count = len(choices)
    last = first + count == BLOCKS
    student_ref = refs.pop(0) if last else None
    state_ref = refs.pop(0) if first else None
    blocks = [[refs.pop(0) for _ in range(n)] for n in choices]
    out_ref = refs.pop(0)
    stats_ref = refs.pop(0) if last else None
    state_vm, total_ref, a_vm, w_vm, a_sem, w_sem, state_sem, *student = refs
    if last:
        state_vm = state_ref
    else:
        total_ref = out_ref
    tok, width = total_ref.shape
    cols = width - 128

    def start(step):
        for off, block in enumerate(blocks[step]):
            wanted = plan_ref[2 * BLOCKS + first + step] == off if len(blocks[step]) > 1 else True

            @pl.when(wanted)
            def _():
                pltpu.make_async_copy(block, a_vm.at[step], a_sem.at[step]).start()

        slot = plan_ref[first + step]

        @pl.when(slot < 8)
        def _():
            pltpu.make_async_copy(near_ref.at[slot], w_vm.at[step], w_sem.at[step]).start()

        @pl.when(slot >= 8)
        def _():
            pltpu.make_async_copy(far_ref.at[slot - 8], w_vm.at[step], w_sem.at[step]).start()

    start(0)
    if first and not last:
        state = pltpu.make_async_copy(state_ref, state_vm, state_sem)
        state.start()
    start(1)
    if last:
        stud_vm, stud_sem = student
        student = pltpu.make_async_copy(student_ref, stud_vm, stud_sem)
        student.start()
    for step in range(count):
        pltpu.make_async_copy(a_vm.at[step], a_vm.at[step], a_sem.at[step]).wait()
        pltpu.make_async_copy(w_vm.at[step], w_vm.at[step], w_sem.at[step]).wait()
        if step + 2 < count:
            start(step + 2)
        final = step == count - 1
        if final and first and not last:
            state.wait()
        if final and last:
            student.wait()
        gain = gain_ref[plan_ref[BLOCKS + first + step]]
        for r in range(0, tok, CHUNK):
            rows = slice(r, r + CHUNK)
            wide = a_vm[step, rows, :].astype(jnp.float32)
            square = wide * wide
            square = square[:, :128] + square[:, 128:256] + square[:, 256:384] + square[:, 384:]
            normed = (wide * gain).astype(jnp.bfloat16)
            total = jnp.dot(normed, w_vm[step], preferred_element_type=jnp.float32)
            if step:
                square += total_ref[rows, cols:]
                total += total_ref[rows, :cols]
            if final and first:
                square += state_vm[rows, cols:]
                total += state_vm[rows, :cols]
            if final and last:
                stats = statistics(total, square, stud_vm[rows, :], out_ref, rows)
                stats_ref[:, rows] = stats
                continue
            total_ref[rows, cols:] = square
            total_ref[rows, :cols] = total


def statistics(logits, square, student, out_ref, rows):
    mean = jnp.sum(square, axis=1, keepdims=True) / (BLOCKS * 512)
    teach = logits * lax.rsqrt(mean + 1e-05)
    out_ref[rows, :] = teach
    stud = student.astype(jnp.float32)
    teach_peak = jnp.max(teach, axis=1, keepdims=True)
    stud_peak = jnp.max(stud, axis=1, keepdims=True)
    teach = teach - teach_peak
    stud = stud - stud_peak
    mass = jnp.exp(stud)
    teach_total = jnp.sum(jnp.exp(teach), axis=1, keepdims=True)
    stud_total = jnp.sum(mass, axis=1, keepdims=True)
    cross = jnp.sum(mass * (stud - teach), axis=1, keepdims=True)
    lane = lax.broadcasted_iota(jnp.int32, (CHUNK, 128), 1)
    packed = jnp.zeros((CHUNK, 128), jnp.float32)
    for at, value in enumerate((teach_peak, teach_total, stud_peak, stud_total, cross)):
        packed = jnp.where(lane == at, value, packed)
    return packed.T[:8, :]


def accumulate_blocks(gain, student, plan, first, blocks, near, far, state=None):
    tok, cols = student.shape
    hbm = pl.BlockSpec(memory_space=pltpu.HBM)
    vmem = pl.BlockSpec(memory_space=pltpu.VMEM)
    smem = pl.BlockSpec(memory_space=pltpu.SMEM)
    logits = jax.ShapeDtypeStruct((tok, cols), jnp.float32)
    totals = jax.ShapeDtypeStruct((tok, cols + 128), jnp.float32)
    stats = jax.ShapeDtypeStruct((8, tok), jnp.float32)
    count = len(blocks)
    last = first + count == BLOCKS
    small = (8, 128)
    scratch = [
        pltpu.VMEM(small if last else totals.shape, jnp.float32),
        pltpu.VMEM(totals.shape if last else small, jnp.float32),
        pltpu.VMEM((count, tok, 512), jnp.bfloat16),
        pltpu.VMEM((count, 512, cols), jnp.bfloat16),
        pltpu.SemaphoreType.DMA((count,)),
        pltpu.SemaphoreType.DMA((count,)),
        pltpu.SemaphoreType.DMA,
    ]
    if last:
        scratch += [pltpu.VMEM((tok, cols), jnp.bfloat16), pltpu.SemaphoreType.DMA]
    parts = [student] * last + [state] * (first > 0) + [one for block in blocks for one in block]
    return pl.pallas_call(
        functools.partial(teacher_kernel, first, [len(block) for block in blocks]),
        out_shape=(logits, stats) if last else totals,
        in_specs=[smem, vmem] + [hbm] * (2 + last) + [vmem] * last + [hbm] * (len(parts) - 2 * last),
        out_specs=(vmem, vmem) if last else vmem,
        scratch_shapes=scratch,
        compiler_params=pltpu.CompilerParams(vmem_limit_bytes=(53 if first else 60) * MIB),
        name="teacher_" + str(first),
    )(plan, gain.reshape(BLOCKS, 1, 512), near, far, *parts)


def merge(first, second):
    teach_peak = jnp.maximum(first[0], second[0])
    stud_peak = jnp.maximum(first[2], second[2])
    teach_total = stud_total = cross = 0.0
    for part in (first, second):
        teach_low = part[0] - teach_peak
        stud_low = part[2] - stud_peak
        weight = jnp.exp(stud_low)
        teach_total = teach_total + jnp.exp(teach_low) * part[1]
        stud_total = stud_total + weight * part[3]
        cross = cross + weight * (part[4] + part[3] * (stud_low - teach_low))
    log_stud = jnp.log(stud_total)
    log_teach = jnp.log(teach_total)
    divergence = cross / stud_total - (log_stud - log_teach)
    offset = (stud_peak - teach_peak) + (log_stud - log_teach) + divergence
    return stud_peak, log_stud, offset, divergence


def combine_kernel(own_ref, near_ref, third_ref, fourth_ref, live_ref, count_ref, coef_ref, sums_ref):
    parts = [
        [ref[at : at + 1, :] for at in range(5)]
        for ref in (own_ref, near_ref, third_ref, fourth_ref)
    ]
    live = live_ref[...]
    stud_peak, log_stud, offset, divergence = merge(parts[0], parts[1])
    other_divergence = merge(parts[2], parts[3])[3]
    coef_ref[...] = jnp.zeros_like(coef_ref)
    coef_ref[0:1, :] = stud_peak
    coef_ref[1:2, :] = log_stud
    coef_ref[2:3, :] = offset
    coef_ref[3:4, :] = V * live
    lane = lax.broadcasted_iota(jnp.int32, (1, 128), 1)
    total = jnp.sum(live * (divergence + other_divergence), axis=1, keepdims=True)
    sums_ref[...] = jnp.where(lane == 0, total, jnp.where(lane == 1, count_ref[0], 0.0))


def combine(stats, others, live, count):
    vmem = pl.BlockSpec(memory_space=pltpu.VMEM)
    return pl.pallas_call(
        combine_kernel,
        out_shape=(
            jax.ShapeDtypeStruct(stats.shape, jnp.float32),
            jax.ShapeDtypeStruct((1, 128), jnp.float32),
        ),
        in_specs=[vmem] * 5 + [pl.BlockSpec(memory_space=pltpu.SMEM)],
        out_specs=(vmem, vmem),
        compiler_params=pltpu.CompilerParams(vmem_limit_bytes=4 * MIB),
        name="combine",
    )(stats, *others, live, count)


def grad_kernel(coef_ref, teach_ref, student_ref, grad_ref):
    coef = coef_ref[...].T
    stud = student_ref[...].astype(jnp.float32)
    prob = jnp.exp((stud - coef[:, 0:1]) - coef[:, 1:2])
    differ = (stud - teach_ref[...]) - coef[:, 2:3]
    grad_ref[...] = ((coef[:, 3:4] * prob) * differ).astype(jnp.bfloat16)


def gradient(coef, teach, student):
    tok, cols = student.shape
    tile = 384
    rows = pl.BlockSpec((tile, cols), lambda i: (i, 0))
    return pl.pallas_call(
        grad_kernel,
        grid=(tok // tile,),
        out_shape=jax.ShapeDtypeStruct((tok, cols), jnp.bfloat16),
        in_specs=[pl.BlockSpec((8, tile), lambda i: (0, i)), rows, rows],
        out_specs=rows,
        compiler_params=pltpu.CompilerParams(vmem_limit_bytes=24 * MIB),
        name="gradient",
    )(coef, teach, student)


def stage(value, axis, moves):
    return sum([lax.ppermute(value, axis, move) for move in moves], value)


def body(teacher_hidden, norm_gain, head_weight, student_logits, row_lengths):
    tok = teacher_hidden.shape[0]
    steps_of = jnp.arange(tok, dtype=jnp.int32) % STEPS
    live = (steps_of < jnp.repeat(row_lengths, STEPS)).astype(jnp.float32)
    count = jnp.sum(row_lengths.astype(jnp.float32))
    accumulate = functools.partial(accumulate_blocks, norm_gain, student_logits, block_plan())
    teach, stats = teacher_logits(head_weight, teacher_hidden, accumulate)
    others = [
        lax.ppermute(stats, "tp", [(t, t ^ m) for t in range(BLOCKS)]) for m in (1, 2, 3)
    ]
    coef, sums = combine(stats, others, live.reshape(1, tok), count.reshape(1))

    sums = stage(sums, "rows", [row_xor(1)])
    sums = stage(sums, "rows", [row_xor(8)])
    grad = gradient(coef, teach, student_logits)
    sums, grad = lax.optimization_barrier((sums, grad))
    sums = stage(sums, "rows", [y_ring(d) for d in (1, 2, 3)])
    sums = stage(sums, "tp", [x_ring(d) for d in (1, 2, 3)])
    loss = sums[0, 0] / (CB * (sums[0, 1] / NX))
    return (grad, loss)


def solution(mesh):
    in_specs = (P("rows", "tp"), P(), P("rows", "tp"), P("rows", "tp"), P("rows"))
    out_specs = (P("rows", "tp"), P())
    return jax.shard_map(body, mesh=mesh, in_specs=in_specs, out_specs=out_specs, check_vma=False)
```

```python
import functools
import itertools

import jax
import jax.numpy as jnp
from jax import lax
from jax.experimental import pallas as pl
from jax.experimental.pallas import tpu as pltpu
from jax.sharding import PartitionSpec as P

V = 2048
CB = 8
STEPS = 4
NX = 4
NZ = 4
NY = 4
NH = 2
BLOCKS = 16
CHUNK = 256
MIB = 1 << 20


def tp_at(x, z):
    return x * NZ + z


def row_at(h, y, c):
    return h * 2 * NY + y * 2 + c


def x_ring(d):
    return [(tp_at(x, z), tp_at((x + d) % NX, z)) for x in range(NX) for z in range(NZ)]


def z_ring(d):
    return [(tp_at(x, z), tp_at(x, (z + d) % NZ)) for x in range(NX) for z in range(NZ)]


def y_ring(d):
    return [
        (row_at(h, y, c), row_at(h, (y + d) % NY, c))
        for h in range(NH)
        for y in range(NY)
        for c in range(2)
    ]


def whole(move):
    places = itertools.product(range(NH), range(NY), range(2), range(NX), range(NZ))

    def at(h, y, c, x, z):
        return row_at(h, y, c) * BLOCKS + tp_at(x, z)

    return [(at(*place), at(*move(*place))) for place in places]


def way(c):
    return 1 - 2 * c


def x_first(h, y, c, x, z):
    return h, y, c, (x + way(c)) % NX, z


def x_second(h, y, c, x, z):
    return h, y, c, (x - way(c)) % NX, z


def z_two(h, y, c, x, z):
    there = (h * NZ + z + 2 * way(c)) % (NH * NZ)
    return there // NZ, y, c, x, there % NZ


def row_xor(m):
    return [(r, r ^ m) for r in range(16)]


SAME_HALF = [[row_at(h, y, c) for y in range(NY) for c in range(2)] for h in range(NH)]


def teacher_logits(weight, own, accumulate):
    def first(value):
        return lax.ppermute(value, ("rows", "tp"), whole(x_first))

    def second(value):
        return lax.ppermute(value, ("rows", "tp"), whole(x_second))

    def far_hop(value):
        return lax.ppermute(value, ("rows", "tp"), whole(z_two))

    def z_hop(value, d):
        return lax.ppermute(value, "tp", z_ring(d))

    def widen(shard):
        return lax.all_gather(shard, "rows", axis_index_groups=SAME_HALF)

    near = widen(weight)
    z1 = z_hop(own, 1)
    half_way = far_hop(weight)
    first0, second0 = first(own), second(own)
    third0 = first(first0)

    here1, half_way, own, *_ = lax.optimization_barrier((z1, half_way, own, second0, third0))
    first1, second1 = first(here1), second(here1)
    third1 = first(first1)
    far = far_hop(half_way)

    far, here1, own, *_ = lax.optimization_barrier((far, here1, own, second1, third1))
    far = widen(far)
    z3 = z_hop(own, -1)

    here3, here1 = lax.optimization_barrier((z3, here1))
    z2 = z_hop(here1, 1)
    first3, second3 = first(here3), second(here3)
    groups = [[own, first0, third0, second0], [here1, first1, third1, second1]]
    state = accumulate(0, [groups[0], groups[0], groups[1], groups[1]], near, near)

    here2, on3, *_ = lax.optimization_barrier((z2, second3, first3, state))
    first2, third3 = first(here2), second(on3)

    here2, on2, *_ = lax.optimization_barrier((here2, first2, third3))
    second2, third2 = second(here2), first(on2)
    blocks = [groups[0], groups[0], groups[1], groups[1]]
    blocks += [[one] for one in (here3, first3, second3, third3, here2, first2)]
    state = accumulate(4, blocks, near, far, state)
    return accumulate(14, [[second2], [third2]], near, far, state)


ORDER = [(0, None), (0, None), (1, None), (1, None)] * 2
ORDER += [(3, 0), (3, 1), (3, 3), (3, 2), (2, 0), (2, 1), (2, 3), (2, 2)]


def block_plan():
    tp = lax.axis_index("tp")
    row = lax.axis_index("rows")
    half = row // 8
    turn = way(row % 2)
    x, z = tp // NZ, tp % NZ
    offsets, blocks, slots = [], [], []
    for step, (i, off) in enumerate(ORDER):
        if off is None:
            side = half if step < 4 else 1 - half
            off = ((x - (2 * side + step % 2)) * turn) % NX
        block = ((x - off * turn) % NX) * NZ + (z - i) % NZ
        offsets.append(jnp.asarray(off, jnp.int32))
        blocks.append(block)
        slots.append(jnp.where(block // 8 == half, block % 8, 8 + block % 8))
    return jnp.stack(slots + blocks + offsets).astype(jnp.int32)


def teacher_kernel(first, choices, plan_ref, gain_ref, near_ref, far_ref, *refs):
    refs = list(refs)
    count = len(choices)
    last = first + count == BLOCKS
    student_ref = refs.pop(0) if last else None
    state_ref = refs.pop(0) if first else None
    blocks = [[refs.pop(0) for _ in range(n)] for n in choices]
    out_ref = refs.pop(0)
    stats_ref = refs.pop(0) if last else None
    total_ref, a_vm, w_vm, a_sem, w_sem, state_sem, *extra = refs
    tok, width = total_ref.shape
    cols = width - 128

    def start(step):
        for off, block in enumerate(blocks[step]):
            wanted = plan_ref[2 * BLOCKS + first + step] == off if len(blocks[step]) > 1 else True

            @pl.when(wanted)
            def _():
                pltpu.make_async_copy(block, a_vm.at[step], a_sem.at[step]).start()

        slot = plan_ref[first + step]

        @pl.when(slot < 8)
        def _():
            pltpu.make_async_copy(near_ref.at[slot], w_vm.at[step], w_sem.at[step]).start()

        @pl.when(slot >= 8)
        def _():
            pltpu.make_async_copy(far_ref.at[slot - 8], w_vm.at[step], w_sem.at[step]).start()

    def multiply(step, r, more=None):
        rows = slice(r, r + CHUNK)
        wide = a_vm[step, rows, :].astype(jnp.float32)
        square = wide * wide
        square = square[:, :128] + square[:, 128:256] + square[:, 256:384] + square[:, 384:]
        normed = (wide * gain_ref[plan_ref[BLOCKS + first + step]]).astype(jnp.bfloat16)
        total = jnp.dot(normed, w_vm[step], preferred_element_type=jnp.float32)
        if more is not None:
            total += more[rows, :cols]
            square += more[rows, cols:]
        return rows, total, square

    def arrive(step):
        pltpu.make_async_copy(a_vm.at[step], a_vm.at[step], a_sem.at[step]).wait()
        pltpu.make_async_copy(w_vm.at[step], w_vm.at[step], w_sem.at[step]).wait()

    def whole_step(step, carry):
        arrive(step)
        for later in range(2, count):

            @pl.when(step + 2 == later)
            def _():
                start(later)

        for r in range(0, tok, CHUNK):
            rows, total, square = multiply(step, r, total_ref)
            total_ref[rows, :cols] = total
            total_ref[rows, cols:] = square
        return carry

    start(0)
    if last:
        state_vm, stud_vm, stud_sem = extra
        student = pltpu.make_async_copy(student_ref, stud_vm, stud_sem)
        state = pltpu.make_async_copy(state_ref.at[pl.ds(0, tok)], state_vm, state_sem)
        start(1)
        state.start()
        student.start()
        arrive(0)
        for r in range(0, tok, CHUNK):
            rows, total, square = multiply(0, r)
            total_ref[rows, :cols] = total
            total_ref[rows, cols:] = square
        arrive(1)
        state.wait()
        student.wait()
        for r in range(0, tok, CHUNK):
            rows, total, square = multiply(1, r, total_ref)
            total += state_vm[rows, :cols]
            square += state_vm[rows, cols:]
            stats_ref[:, rows] = statistics(total, square, stud_vm[rows, :], out_ref, rows)
        return
    if first:
        state = pltpu.make_async_copy(state_ref.at[pl.ds(0, tok)], total_ref, state_sem)
        state.start()
        start(1)
        state.wait()
    else:
        start(1)
        total_ref[...] = jnp.zeros_like(total_ref)
    lax.fori_loop(0, count, whole_step, 0)
    result = pltpu.make_async_copy(total_ref, out_ref.at[pl.ds(0, tok)], state_sem)
    result.start()
    result.wait()


def statistics(logits, square, student, out_ref, rows):
    mean = jnp.sum(square, axis=1, keepdims=True) / (BLOCKS * 512)
    teach = logits * lax.rsqrt(mean + 1e-05)
    out_ref[rows, :] = teach
    stud = student.astype(jnp.float32)
    teach_peak = jnp.max(teach, axis=1, keepdims=True)
    stud_peak = jnp.max(stud, axis=1, keepdims=True)
    teach = teach - teach_peak
    stud = stud - stud_peak
    mass = jnp.exp(stud)
    teach_total = jnp.sum(jnp.exp(teach), axis=1, keepdims=True)
    stud_total = jnp.sum(mass, axis=1, keepdims=True)
    cross = jnp.sum(mass * (stud - teach), axis=1, keepdims=True)
    lane = lax.broadcasted_iota(jnp.int32, (CHUNK, 128), 1)
    packed = jnp.zeros((CHUNK, 128), jnp.float32)
    for at, value in enumerate((teach_peak, teach_total, stud_peak, stud_total, cross)):
        packed = jnp.where(lane == at, value, packed)
    return packed.T[:8, :]


def accumulate_blocks(gain, student, plan, first, blocks, near, far, state=None):
    tok, cols = student.shape
    hbm = pl.BlockSpec(memory_space=pltpu.HBM)
    vmem = pl.BlockSpec(memory_space=pltpu.VMEM)
    smem = pl.BlockSpec(memory_space=pltpu.SMEM)
    anywhere = pl.BlockSpec(memory_space=pl.ANY)
    logits = jax.ShapeDtypeStruct((tok, cols), jnp.float32)
    totals = jax.ShapeDtypeStruct((8 * tok, cols + 128), jnp.float32)
    stats = jax.ShapeDtypeStruct((8, tok), jnp.float32)
    count = len(blocks)
    last = first + count == BLOCKS
    scratch = [
        pltpu.VMEM((tok, cols + 128), jnp.float32),
        pltpu.VMEM((count, tok, 512), jnp.bfloat16),
        pltpu.VMEM((count, 512, cols), jnp.bfloat16),
        pltpu.SemaphoreType.DMA((count,)),
        pltpu.SemaphoreType.DMA((count,)),
        pltpu.SemaphoreType.DMA,
    ]
    if last:
        scratch += [
            pltpu.VMEM((tok, cols + 128), jnp.float32),
            pltpu.VMEM((tok, cols), jnp.bfloat16),
            pltpu.SemaphoreType.DMA,
        ]
    parts = [student] * last + [state] * (first > 0) + [one for block in blocks for one in block]
    return pl.pallas_call(
        functools.partial(teacher_kernel, first, [len(block) for block in blocks]),
        out_shape=(logits, stats) if last else totals,
        in_specs=[smem, vmem] + [hbm] * 2 + [anywhere] * len(parts),
        out_specs=(vmem, vmem) if last else hbm,
        scratch_shapes=scratch,
        compiler_params=pltpu.CompilerParams(vmem_limit_bytes=(42 if last else 60) * MIB),
        name="teacher_" + str(first),
    )(plan, gain.reshape(BLOCKS, 1, 512), near, far, *parts)


def merge(first, second):
    teach_peak = jnp.maximum(first[0], second[0])
    stud_peak = jnp.maximum(first[2], second[2])
    teach_total = stud_total = cross = 0.0
    for part in (first, second):
        teach_low = part[0] - teach_peak
        stud_low = part[2] - stud_peak
        weight = jnp.exp(stud_low)
        teach_total = teach_total + jnp.exp(teach_low) * part[1]
        stud_total = stud_total + weight * part[3]
        cross = cross + weight * (part[4] + part[3] * (stud_low - teach_low))
    log_stud = jnp.log(stud_total)
    log_teach = jnp.log(teach_total)
    divergence = cross / stud_total - (log_stud - log_teach)
    offset = (stud_peak - teach_peak) + (log_stud - log_teach) + divergence
    return stud_peak, log_stud, offset, divergence


def combine_kernel(own_ref, near_ref, third_ref, fourth_ref, live_ref, count_ref, coef_ref, sums_ref):
    parts = [
        [ref[at : at + 1, :] for at in range(5)]
        for ref in (own_ref, near_ref, third_ref, fourth_ref)
    ]
    live = live_ref[...]
    stud_peak, log_stud, offset, divergence = merge(parts[0], parts[1])
    other_divergence = merge(parts[2], parts[3])[3]
    coef_ref[...] = jnp.zeros_like(coef_ref)
    coef_ref[0:1, :] = stud_peak
    coef_ref[1:2, :] = log_stud
    coef_ref[2:3, :] = offset
    coef_ref[3:4, :] = V * live
    lane = lax.broadcasted_iota(jnp.int32, (1, 128), 1)
    total = jnp.sum(live * (divergence + other_divergence), axis=1, keepdims=True)
    sums_ref[...] = jnp.where(lane == 0, total, jnp.where(lane == 1, count_ref[0], 0.0))


def combine(stats, others, live, count):
    vmem = pl.BlockSpec(memory_space=pltpu.VMEM)
    return pl.pallas_call(
        combine_kernel,
        out_shape=(
            jax.ShapeDtypeStruct(stats.shape, jnp.float32),
            jax.ShapeDtypeStruct((1, 128), jnp.float32),
        ),
        in_specs=[vmem] * 5 + [pl.BlockSpec(memory_space=pltpu.SMEM)],
        out_specs=(vmem, vmem),
        compiler_params=pltpu.CompilerParams(vmem_limit_bytes=4 * MIB),
        name="combine",
    )(stats, *others, live, count)


def grad_kernel(coef_ref, teach_ref, student_ref, grad_ref):
    coef = coef_ref[...].T
    stud = student_ref[...].astype(jnp.float32)
    prob = jnp.exp((stud - coef[:, 0:1]) - coef[:, 1:2])
    differ = (stud - teach_ref[...]) - coef[:, 2:3]
    grad_ref[...] = ((coef[:, 3:4] * prob) * differ).astype(jnp.bfloat16)


def gradient(coef, teach, student):
    tok, cols = student.shape
    tile = 384
    rows = pl.BlockSpec((tile, cols), lambda i: (i, 0))
    return pl.pallas_call(
        grad_kernel,
        grid=(tok // tile,),
        out_shape=jax.ShapeDtypeStruct((tok, cols), jnp.bfloat16),
        in_specs=[pl.BlockSpec((8, tile), lambda i: (0, i)), rows, rows],
        out_specs=rows,
        compiler_params=pltpu.CompilerParams(vmem_limit_bytes=24 * MIB),
        name="gradient",
    )(coef, teach, student)


def stage(value, axis, moves):
    return sum([lax.ppermute(value, axis, move) for move in moves], value)


def body(teacher_hidden, norm_gain, head_weight, student_logits, row_lengths):
    tok = teacher_hidden.shape[0]
    steps_of = jnp.arange(tok, dtype=jnp.int32) % STEPS
    live = (steps_of < jnp.repeat(row_lengths, STEPS)).astype(jnp.float32)
    count = jnp.sum(row_lengths.astype(jnp.float32))
    accumulate = functools.partial(accumulate_blocks, norm_gain, student_logits, block_plan())
    teach, stats = teacher_logits(head_weight, teacher_hidden, accumulate)
    others = [
        lax.ppermute(stats, "tp", [(t, t ^ m) for t in range(BLOCKS)]) for m in (1, 2, 3)
    ]
    coef, sums = combine(stats, others, live.reshape(1, tok), count.reshape(1))

    sums = stage(sums, "rows", [row_xor(1)])
    sums = stage(sums, "rows", [row_xor(8)])
    grad = gradient(coef, teach, student_logits)
    sums, grad = lax.optimization_barrier((sums, grad))
    sums = stage(sums, "rows", [y_ring(d) for d in (1, 2, 3)])
    sums = stage(sums, "tp", [x_ring(d) for d in (1, 2, 3)])
    loss = sums[0, 0] / (CB * (sums[0, 1] / NX))
    return (grad, loss)


def solution(mesh):
    in_specs = (P("rows", "tp"), P(), P("rows", "tp"), P("rows", "tp"), P("rows"))
    out_specs = (P("rows", "tp"), P())
    return jax.shard_map(body, mesh=mesh, in_specs=in_specs, out_specs=out_specs, check_vma=False)
```

```python
import functools
import itertools

import jax
import jax.numpy as jnp
from jax import lax
from jax.experimental import pallas as pl
from jax.experimental.pallas import tpu as pltpu
from jax.sharding import PartitionSpec as P

V = 2048
CB = 8
STEPS = 4
NX = 4
NZ = 4
NY = 4
NH = 2
BLOCKS = 16
CHUNK = 128
MIB = 1 << 20


def tp_at(x, z):
    return x * NZ + z


def row_at(h, y, c):
    return h * 2 * NY + y * 2 + c


def x_ring(d):
    return [(tp_at(x, z), tp_at((x + d) % NX, z)) for x in range(NX) for z in range(NZ)]


def z_ring(d):
    return [(tp_at(x, z), tp_at(x, (z + d) % NZ)) for x in range(NX) for z in range(NZ)]


def y_ring(d):
    return [
        (row_at(h, y, c), row_at(h, (y + d) % NY, c))
        for h in range(NH)
        for y in range(NY)
        for c in range(2)
    ]


def whole(move):
    places = itertools.product(range(NH), range(NY), range(2), range(NX), range(NZ))

    def at(h, y, c, x, z):
        return row_at(h, y, c) * BLOCKS + tp_at(x, z)

    return [(at(*place), at(*move(*place))) for place in places]


def way(c):
    return 1 - 2 * c


def x_first(h, y, c, x, z):
    return h, y, c, (x + way(c)) % NX, z


def x_second(h, y, c, x, z):
    return h, y, c, (x - way(c)) % NX, z


def y_first(h, y, c, x, z):
    return h, (y + way(c)) % NY, c, x, z


def y_second(h, y, c, x, z):
    return h, (y - way(c)) % NY, c, x, z


def other_core(h, y, c, x, z):
    return h, y, 1 - c, x, z


def z_two(h, y, c, x, z):
    there = (h * NZ + z + 2 * way(c)) % (NH * NZ)
    return there // NZ, y, c, x, there % NZ


def row_xor(m):
    return [(r, r ^ m) for r in range(16)]


def teacher_logits(weight, own, accumulate):
    def go(move):
        pairs = whole(move)
        return lambda value: lax.ppermute(value, ("rows", "tp"), pairs)

    first, second, far_hop = go(x_first), go(x_second), go(z_two)
    y_one, y_two, swap = go(y_first), go(y_second), go(other_core)

    def z_hop(value, d):
        return lax.ppermute(value, "tp", z_ring(d))

    z1 = z_hop(own, 1)
    half_way = far_hop(weight)
    first0, second0 = first(own), second(own)
    near1, near3 = y_one(weight), y_two(weight)
    third0 = first(first0)

    other0 = swap(weight)

    here1, half_way, own, near1, near3, *_ = lax.optimization_barrier(
        (z1, half_way, own, near1, near3, second0, third0, other0)
    )
    first1, second1 = first(here1), second(here1)
    near2 = y_one(near1)
    other1 = swap(near1)
    far0 = far_hop(half_way)

    far0, here1, own, on1, near2, near3, *_ = lax.optimization_barrier(
        (far0, here1, own, first1, near2, near3, second1, other1)
    )
    z3 = z_hop(own, -1)
    third1 = first(on1)
    other2, other3, other4 = swap(near2), swap(near3), swap(far0)

    here3, here1, far0, third1, *_ = lax.optimization_barrier(
        (z3, here1, far0, third1, other2, other3, other4)
    )
    far1, far3 = y_one(far0), y_two(far0)
    z2 = z_hop(here1, 1)
    first3, second3 = first(here3), second(here3)
    groups = [[own, first0, third0, second0], [here1, first1, third1, second1]]
    blocks = [groups[0], groups[0], groups[1], groups[1]]
    near = [weight, near1, near2, near3, other0, other1, other2, other3]
    (state,) = accumulate(0, blocks, near)

    here2, on3, far1, far3, *_ = lax.optimization_barrier(
        (z2, second3, far1, far3, first3, state)
    )
    first2, third3 = first(here2), second(on3)
    far2 = y_one(far1)
    other5, other7 = swap(far1), swap(far3)

    here2, on2, far2, *_ = lax.optimization_barrier(
        (here2, first2, far2, third3, other5, other7)
    )
    second2, third2 = second(here2), first(on2)
    other6 = swap(far2)
    blocks += [[one] for one in (here3, first3, second3, third3, here2, first2)]
    far = [far0, far1, far2, far3, other4, other5, other6, other7]
    state, picked = accumulate(4, blocks, near + far, state)
    return accumulate(14, [[second2], [third2]], [picked], state)


ORDER = [(0, None), (0, None), (1, None), (1, None)] * 2
ORDER += [(3, 0), (3, 1), (3, 3), (3, 2), (2, 0), (2, 1), (2, 3), (2, 2)]


def block_plan():
    tp = lax.axis_index("tp")
    row = lax.axis_index("rows")
    half = row // 8
    turn = way(row % 2)
    x, z = tp // NZ, tp % NZ
    offsets, blocks, slots = [], [], []
    for step, (i, off) in enumerate(ORDER):
        if off is None:
            side = half if step < 4 else 1 - half
            off = ((x - (2 * side + step % 2)) * turn) % NX
        block = ((x - off * turn) % NX) * NZ + (z - i) % NZ
        offsets.append(jnp.asarray(off, jnp.int32))
        blocks.append(block)
        same = block % 2 == row % 2
        y_off = ((row % 8 // 2 - block % 8 // 2) * jnp.where(same, turn, -turn)) % NY
        slots.append(jnp.where(block // 8 == half, 0, 8) + jnp.where(same, 0, 4) + y_off)
    return jnp.stack(slots + blocks + offsets).astype(jnp.int32)


def teacher_kernel(first, choices, n_weights, plan_ref, gain_ref, *refs):
    refs = list(refs)
    count = len(choices)
    last = first + count == BLOCKS
    student_ref = refs.pop(0) if last else None
    state_ref = refs.pop(0) if first else None
    weights = [refs.pop(0) for _ in range(n_weights)]
    blocks = [[refs.pop(0) for _ in range(n)] for n in choices]
    out_ref = refs.pop(0)
    stats_ref = refs.pop(0) if last else None
    picked_ref = refs.pop(0) if first and not last else None
    total_ref, a_vm, w_vm, a_sem, w_sem, state_sem, out_sem, *extra = refs
    tok, width = total_ref.shape
    cols = width - 128

    def start_block(step):
        for off, block in enumerate(blocks[step]):
            wanted = plan_ref[2 * BLOCKS + first + step] == off if len(blocks[step]) > 1 else True

            @pl.when(wanted)
            def _():
                pltpu.make_async_copy(block, a_vm.at[step], a_sem.at[step]).start()

    def start_weights(step, carry=0):
        to, sem = w_vm.at[step], w_sem.at[step]
        if last:
            pltpu.make_async_copy(weights[0].at[step], to, sem).start()
            return carry
        slot = plan_ref[first + step]
        for at, ref in enumerate(weights):

            @pl.when(slot == at)
            def _():
                pltpu.make_async_copy(ref, to, sem).start()

        return carry

    def each_chunk(do):
        if picked_ref is not None:
            for at in range(0, tok, 2 * CHUNK):
                do(pl.ds(at, 2 * CHUNK))
            return

        def one(at, carry):
            do(pl.ds(pl.multiple_of(at * CHUNK, CHUNK), CHUNK))
            return carry

        lax.fori_loop(0, tok // CHUNK, one, 0)

    def multiply(step, rows, more=None):
        wide = a_vm[step, rows, :].astype(jnp.float32)
        square = wide * wide
        square = square[:, :128] + square[:, 128:256] + square[:, 256:384] + square[:, 384:]
        normed = (wide * gain_ref[plan_ref[BLOCKS + first + step]]).astype(jnp.bfloat16)
        total = jnp.dot(normed, w_vm[step], preferred_element_type=jnp.float32)
        if more is not None:
            total += more[rows, :cols]
            square += more[rows, cols:]
        return total, square

    def arrive(step):
        pltpu.make_async_copy(a_vm.at[step], a_vm.at[step], a_sem.at[step]).wait()
        pltpu.make_async_copy(w_vm.at[step], w_vm.at[step], w_sem.at[step]).wait()

    def whole_step(step, carry):
        arrive(step)
        for later in range(2, count):

            @pl.when(step + 2 == later)
            def _():
                start_block(later)

        @pl.when(step + 2 < count)
        def _():
            start_weights(step + 2)

        if picked_ref is not None:

            @pl.when((step == 2) | (step == 3))
            def _():
                start_weights(count + step - 2)

            @pl.when(step == 6)
            def _():
                for at in range(2):
                    pick = w_vm.at[count + at]
                    sem = w_sem.at[count + at]
                    pltpu.make_async_copy(pick, pick, sem).wait()
                    pltpu.make_async_copy(pick, picked_ref.at[at], sem).start()

        def add(rows):
            total, square = multiply(step, rows, total_ref)
            total_ref[rows, :cols] = total
            total_ref[rows, cols:] = square

        each_chunk(add)
        return carry

    start_block(0)
    start_block(1)
    lax.fori_loop(0, 2, start_weights, 0)
    if last:
        state_vm, stud_vm, stud_sem = extra
        student = pltpu.make_async_copy(student_ref, stud_vm, stud_sem)
        state = pltpu.make_async_copy(state_ref.at[pl.ds(0, tok)], state_vm, state_sem)
        state.start()
        student.start()
        arrive(0)

        def begin(rows):
            total, square = multiply(0, rows)
            total_ref[rows, :cols] = total
            total_ref[rows, cols:] = square

        each_chunk(begin)
        arrive(1)
        state.wait()
        student.wait()

        def finish(rows):
            total, square = multiply(1, rows, total_ref)
            total += state_vm[rows, :cols]
            square += state_vm[rows, cols:]
            stats_ref[:, rows] = statistics(total, square, stud_vm[rows, :], out_ref, rows)

        each_chunk(finish)
        return
    if first:
        state = pltpu.make_async_copy(state_ref.at[pl.ds(0, tok)], extra[0], state_sem)
        state.start()
    total_ref[...] = jnp.zeros_like(total_ref)
    lax.fori_loop(0, count, whole_step, 0)
    if first:
        state.wait()
    copies = []
    for r in range(0, tok, CHUNK):
        rows = pl.ds(r, CHUNK)
        if first:
            total_ref[rows, :] += extra[0][rows, :]
        copies.append(
            pltpu.make_async_copy(total_ref.at[rows], out_ref.at[rows], out_sem.at[r // CHUNK])
        )
        copies[-1].start()
    if picked_ref is not None:
        for at in range(2):
            copies.append(
                pltpu.make_async_copy(
                    w_vm.at[count + at], picked_ref.at[at], w_sem.at[count + at]
                )
            )
    for copy in copies:
        copy.wait()


def statistics(logits, square, student, out_ref, rows):
    mean = jnp.sum(square, axis=1, keepdims=True) / (BLOCKS * 512)
    teach = logits * lax.rsqrt(mean + 1e-05)
    out_ref[rows, :] = teach
    stud = student.astype(jnp.float32)
    teach_peak = jnp.max(teach, axis=1, keepdims=True)
    stud_peak = jnp.max(stud, axis=1, keepdims=True)
    teach = teach - teach_peak
    stud = stud - stud_peak
    mass = jnp.exp(stud)
    teach_total = jnp.sum(jnp.exp(teach), axis=1, keepdims=True)
    stud_total = jnp.sum(mass, axis=1, keepdims=True)
    cross = jnp.sum(mass * (stud - teach), axis=1, keepdims=True)
    lane = lax.broadcasted_iota(jnp.int32, (CHUNK, 128), 1)
    packed = jnp.zeros((CHUNK, 128), jnp.float32)
    for at, value in enumerate((teach_peak, teach_total, stud_peak, stud_total, cross)):
        packed = jnp.where(lane == at, value, packed)
    return packed.T[:8, :]


def accumulate_blocks(gain, student, plan, first, blocks, weights, state=None):
    tok, cols = student.shape
    hbm = pl.BlockSpec(memory_space=pltpu.HBM)
    vmem = pl.BlockSpec(memory_space=pltpu.VMEM)
    smem = pl.BlockSpec(memory_space=pltpu.SMEM)
    anywhere = pl.BlockSpec(memory_space=pl.ANY)
    logits = jax.ShapeDtypeStruct((tok, cols), jnp.float32)
    totals = jax.ShapeDtypeStruct(((8 if first else 1) * tok, cols + 128), jnp.float32)
    picked = jax.ShapeDtypeStruct((24, 512, cols), jnp.bfloat16)
    stats = jax.ShapeDtypeStruct((8, tok), jnp.float32)
    count = len(blocks)
    last = first + count == BLOCKS
    scratch = [
        pltpu.VMEM((tok, cols + 128), jnp.float32),
        pltpu.VMEM((count, tok, 512), jnp.bfloat16),
        pltpu.VMEM((count + 2, 512, cols), jnp.bfloat16),
        pltpu.SemaphoreType.DMA((count,)),
        pltpu.SemaphoreType.DMA((count + 2,)),
        pltpu.SemaphoreType.DMA,
        pltpu.SemaphoreType.DMA((tok // CHUNK,)),
    ]
    if first:
        scratch += [pltpu.VMEM((tok, cols + 128), jnp.float32)]
    if last:
        scratch += [
            pltpu.VMEM((tok, cols), jnp.bfloat16),
            pltpu.SemaphoreType.DMA,
        ]
    parts = [student] * last + [state] * (first > 0) + weights
    parts += [one for block in blocks for one in block]
    return pl.pallas_call(
        functools.partial(teacher_kernel, first, [len(block) for block in blocks], len(weights)),
        out_shape=(logits, stats) if last else (totals, picked) if first else (totals,),
        in_specs=[smem, vmem] + [anywhere] * len(parts),
        out_specs=(vmem, vmem) if last else (hbm, hbm) if first else (hbm,),
        scratch_shapes=scratch,
        compiler_params=pltpu.CompilerParams(vmem_limit_bytes=(42 if last else 60) * MIB),
        name="teacher_" + str(first),
    )(plan, gain.reshape(BLOCKS, 1, 512), *parts)


def merge(first, second):
    teach_peak = jnp.maximum(first[0], second[0])
    stud_peak = jnp.maximum(first[2], second[2])
    teach_total = stud_total = cross = 0.0
    for part in (first, second):
        teach_low = part[0] - teach_peak
        stud_low = part[2] - stud_peak
        weight = jnp.exp(stud_low)
        teach_total = teach_total + jnp.exp(teach_low) * part[1]
        stud_total = stud_total + weight * part[3]
        cross = cross + weight * (part[4] + part[3] * (stud_low - teach_low))
    log_stud = jnp.log(stud_total)
    log_teach = jnp.log(teach_total)
    divergence = cross / stud_total - (log_stud - log_teach)
    offset = (stud_peak - teach_peak) + (log_stud - log_teach) + divergence
    return stud_peak, log_stud, offset, divergence


def combine_kernel(own_ref, near_ref, third_ref, fourth_ref, live_ref, count_ref, coef_ref, sums_ref):
    parts = [
        [ref[at : at + 1, :] for at in range(5)]
        for ref in (own_ref, near_ref, third_ref, fourth_ref)
    ]
    live = live_ref[...]
    stud_peak, log_stud, offset, divergence = merge(parts[0], parts[1])
    other_divergence = merge(parts[2], parts[3])[3]
    coef_ref[...] = jnp.zeros_like(coef_ref)
    coef_ref[0:1, :] = stud_peak
    coef_ref[1:2, :] = log_stud
    coef_ref[2:3, :] = offset
    coef_ref[3:4, :] = V * live
    lane = lax.broadcasted_iota(jnp.int32, (1, 128), 1)
    total = jnp.sum(live * (divergence + other_divergence), axis=1, keepdims=True)
    sums_ref[...] = jnp.where(lane == 0, total, jnp.where(lane == 1, count_ref[0], 0.0))


def combine(stats, others, live, count):
    vmem = pl.BlockSpec(memory_space=pltpu.VMEM)
    return pl.pallas_call(
        combine_kernel,
        out_shape=(
            jax.ShapeDtypeStruct(stats.shape, jnp.float32),
            jax.ShapeDtypeStruct((1, 128), jnp.float32),
        ),
        in_specs=[vmem] * 5 + [pl.BlockSpec(memory_space=pltpu.SMEM)],
        out_specs=(vmem, vmem),
        compiler_params=pltpu.CompilerParams(vmem_limit_bytes=4 * MIB),
        name="combine",
    )(stats, *others, live, count)


def grad_kernel(coef_ref, teach_ref, student_ref, grad_ref):
    def one(at, carry):
        rows = pl.ds(pl.multiple_of(at * CHUNK, CHUNK), CHUNK)
        coef = coef_ref[:, rows].T
        stud = student_ref[rows, :].astype(jnp.float32)
        prob = jnp.exp((stud - coef[:, 0:1]) - coef[:, 1:2])
        differ = (stud - teach_ref[rows, :]) - coef[:, 2:3]
        grad_ref[rows, :] = ((coef[:, 3:4] * prob) * differ).astype(jnp.bfloat16)
        return carry

    lax.fori_loop(0, student_ref.shape[0] // CHUNK, one, 0)


def gradient(coef, teach, student):
    tok, cols = student.shape
    tile = 384
    rows = pl.BlockSpec((tile, cols), lambda i: (i, 0))
    return pl.pallas_call(
        grad_kernel,
        grid=(tok // tile,),
        out_shape=jax.ShapeDtypeStruct((tok, cols), jnp.bfloat16),
        in_specs=[pl.BlockSpec((8, tile), lambda i: (0, i)), rows, rows],
        out_specs=rows,
        compiler_params=pltpu.CompilerParams(vmem_limit_bytes=24 * MIB),
        name="gradient",
    )(coef, teach, student)


def stage(value, axis, moves):
    return sum([lax.ppermute(value, axis, move) for move in moves], value)


def body(teacher_hidden, norm_gain, head_weight, student_logits, row_lengths):
    tok = teacher_hidden.shape[0]
    steps_of = jnp.arange(tok, dtype=jnp.int32) % STEPS
    live = (steps_of < jnp.repeat(row_lengths, STEPS)).astype(jnp.float32)
    count = jnp.sum(row_lengths.astype(jnp.float32))
    accumulate = functools.partial(accumulate_blocks, norm_gain, student_logits, block_plan())
    teach, stats = teacher_logits(head_weight, teacher_hidden, accumulate)
    others = [
        lax.ppermute(stats, "tp", [(t, t ^ m) for t in range(BLOCKS)]) for m in (1, 2, 3)
    ]
    coef, sums = combine(stats, others, live.reshape(1, tok), count.reshape(1))

    sums = stage(sums, "rows", [row_xor(1)])
    sums = stage(sums, "rows", [row_xor(8)])
    grad = gradient(coef, teach, student_logits)
    sums, grad = lax.optimization_barrier((sums, grad))
    sums = stage(sums, "rows", [y_ring(d) for d in (1, 2, 3)])
    sums = stage(sums, "tp", [x_ring(d) for d in (1, 2, 3)])
    loss = sums[0, 0] / (CB * (sums[0, 1] / NX))
    return (grad, loss)


def solution(mesh):
    in_specs = (P("rows", "tp"), P(), P("rows", "tp"), P("rows", "tp"), P("rows"))
    out_specs = (P("rows", "tp"), P())
    return jax.shard_map(body, mesh=mesh, in_specs=in_specs, out_specs=out_specs, check_vma=False)
```

```python
import functools
import itertools

import jax
import jax.numpy as jnp
from jax import lax
from jax.experimental import pallas as pl
from jax.experimental.pallas import tpu as pltpu
from jax.sharding import PartitionSpec as P

V = 2048
CB = 8
STEPS = 4
NX = 4
NZ = 4
NY = 4
NH = 2
BLOCKS = 16
CHUNK = 256
MIB = 1 << 20


def tp_at(x, z):
    return x * NZ + z


def row_at(h, y, c):
    return h * 2 * NY + y * 2 + c


def x_ring(d):
    return [(tp_at(x, z), tp_at((x + d) % NX, z)) for x in range(NX) for z in range(NZ)]


def z_ring(d):
    return [(tp_at(x, z), tp_at(x, (z + d) % NZ)) for x in range(NX) for z in range(NZ)]


def y_ring(d):
    return [
        (row_at(h, y, c), row_at(h, (y + d) % NY, c))
        for h in range(NH)
        for y in range(NY)
        for c in range(2)
    ]


def whole(move):
    places = itertools.product(range(NH), range(NY), range(2), range(NX), range(NZ))

    def at(h, y, c, x, z):
        return row_at(h, y, c) * BLOCKS + tp_at(x, z)

    return [(at(*place), at(*move(*place))) for place in places]


def way(c):
    return 1 - 2 * c


def x_first(h, y, c, x, z):
    return h, y, c, (x + way(c)) % NX, z


def x_second(h, y, c, x, z):
    return h, y, c, (x - way(c)) % NX, z


def z_two(h, y, c, x, z):
    there = (h * NZ + z + 2 * way(c)) % (NH * NZ)
    return there // NZ, y, c, x, there % NZ


def row_xor(m):
    return [(r, r ^ m) for r in range(16)]


SAME_HALF = [[row_at(h, y, c) for y in range(NY) for c in range(2)] for h in range(NH)]


def teacher_logits(weight, own, accumulate):
    def first(value):
        return lax.ppermute(value, ("rows", "tp"), whole(x_first))

    def second(value):
        return lax.ppermute(value, ("rows", "tp"), whole(x_second))

    def far_hop(value):
        return lax.ppermute(value, ("rows", "tp"), whole(z_two))

    def z_hop(value, d):
        return lax.ppermute(value, "tp", z_ring(d))

    def widen(shard):
        return lax.all_gather(shard, "rows", axis_index_groups=SAME_HALF)

    near = widen(weight)
    z1 = z_hop(own, 1)
    half_way = far_hop(weight)
    first0, second0 = first(own), second(own)
    third0 = first(first0)

    here1, half_way, own, *_ = lax.optimization_barrier((z1, half_way, own, second0, third0))
    first1, second1 = first(here1), second(here1)
    far = far_hop(half_way)

    far, here1, own, on1, *_ = lax.optimization_barrier((far, here1, own, first1, second1))
    far = widen(far)
    z3 = z_hop(own, -1)
    third1 = first(on1)

    here3, here1, third1 = lax.optimization_barrier((z3, here1, third1))
    z2 = z_hop(here1, 1)
    first3, second3 = first(here3), second(here3)
    groups = [[own, first0, third0, second0], [here1, first1, third1, second1]]
    state = accumulate(0, [groups[0], groups[0], groups[1], groups[1]], near, near)

    here2, on3, *_ = lax.optimization_barrier((z2, second3, first3, state))
    first2, third3 = first(here2), second(on3)

    here2, on2, *_ = lax.optimization_barrier((here2, first2, third3))
    second2, third2 = second(here2), first(on2)
    blocks = [groups[0], groups[0], groups[1], groups[1]]
    blocks += [[one] for one in (here3, first3, second3, third3, here2, first2)]
    state = accumulate(4, blocks, near, far, state)
    return accumulate(14, [[second2], [third2]], near, far, state)


ORDER = [(0, None), (0, None), (1, None), (1, None)] * 2
ORDER += [(3, 0), (3, 1), (3, 3), (3, 2), (2, 0), (2, 1), (2, 3), (2, 2)]


def block_plan():
    tp = lax.axis_index("tp")
    row = lax.axis_index("rows")
    half = row // 8
    turn = way(row % 2)
    x, z = tp // NZ, tp % NZ
    offsets, blocks, slots = [], [], []
    for step, (i, off) in enumerate(ORDER):
        if off is None:
            side = half if step < 4 else 1 - half
            off = ((x - (2 * side + step % 2)) * turn) % NX
        block = ((x - off * turn) % NX) * NZ + (z - i) % NZ
        offsets.append(jnp.asarray(off, jnp.int32))
        blocks.append(block)
        slots.append(jnp.where(block // 8 == half, block % 8, 8 + block % 8))
    return jnp.stack(slots + blocks + offsets).astype(jnp.int32)


def teacher_kernel(first, choices, plan_ref, gain_ref, near_ref, far_ref, *refs):
    refs = list(refs)
    count = len(choices)
    last = first + count == BLOCKS
    student_ref = refs.pop(0) if last else None
    state_ref = refs.pop(0) if first else None
    blocks = [[refs.pop(0) for _ in range(n)] for n in choices]
    out_ref = refs.pop(0)
    stats_ref = refs.pop(0) if last else None
    total_ref, a_vm, w_vm, a_sem, w_sem, state_sem, out_sem, *extra = refs
    tok, width = total_ref.shape
    cols = width - 128

    def start(step):
        for off, block in enumerate(blocks[step]):
            wanted = plan_ref[2 * BLOCKS + first + step] == off if len(blocks[step]) > 1 else True

            @pl.when(wanted)
            def _():
                pltpu.make_async_copy(block, a_vm.at[step], a_sem.at[step]).start()

        slot = plan_ref[first + step]

        @pl.when(slot < 8)
        def _():
            pltpu.make_async_copy(near_ref.at[slot], w_vm.at[step], w_sem.at[step]).start()

        @pl.when(slot >= 8)
        def _():
            pltpu.make_async_copy(far_ref.at[slot - 8], w_vm.at[step], w_sem.at[step]).start()

    def multiply(step, r, more=None):
        rows = slice(r, r + CHUNK)
        wide = a_vm[step, rows, :].astype(jnp.float32)
        square = wide * wide
        square = square[:, :128] + square[:, 128:256] + square[:, 256:384] + square[:, 384:]
        normed = (wide * gain_ref[plan_ref[BLOCKS + first + step]]).astype(jnp.bfloat16)
        total = jnp.dot(normed, w_vm[step], preferred_element_type=jnp.float32)
        if more is not None:
            total += more[rows, :cols]
            square += more[rows, cols:]
        return rows, total, square

    def arrive(step):
        pltpu.make_async_copy(a_vm.at[step], a_vm.at[step], a_sem.at[step]).wait()
        pltpu.make_async_copy(w_vm.at[step], w_vm.at[step], w_sem.at[step]).wait()

    def whole_step(step, carry):
        arrive(step)
        for later in range(2, count):

            @pl.when(step + 2 == later)
            def _():
                start(later)

        for r in range(0, tok, CHUNK):
            rows, total, square = multiply(step, r, total_ref)
            total_ref[rows, :cols] = total
            total_ref[rows, cols:] = square
        return carry

    start(0)
    if last:
        state_vm, stud_vm, stud_sem = extra
        student = pltpu.make_async_copy(student_ref, stud_vm, stud_sem)
        state = pltpu.make_async_copy(state_ref.at[pl.ds(0, tok)], state_vm, state_sem)
        start(1)
        state.start()
        student.start()
        arrive(0)
        for r in range(0, tok, CHUNK):
            rows, total, square = multiply(0, r)
            total_ref[rows, :cols] = total
            total_ref[rows, cols:] = square
        arrive(1)
        state.wait()
        student.wait()
        for r in range(0, tok, CHUNK):
            rows, total, square = multiply(1, r, total_ref)
            total += state_vm[rows, :cols]
            square += state_vm[rows, cols:]
            stats_ref[:, rows] = statistics(total, square, stud_vm[rows, :], out_ref, rows)
        return
    start(1)
    if first:
        (state_vm,) = extra
        state = pltpu.make_async_copy(state_ref.at[pl.ds(0, tok)], state_vm, state_sem)
        state.start()
    total_ref[...] = jnp.zeros_like(total_ref)
    lax.fori_loop(0, count, whole_step, 0)
    if first:
        state.wait()
    copies = []
    for r in range(0, tok, CHUNK):
        rows = pl.ds(r, CHUNK)
        if first:
            total_ref[rows, :] += state_vm[rows, :]
        copies.append(
            pltpu.make_async_copy(total_ref.at[rows], out_ref.at[rows], out_sem.at[r // CHUNK])
        )
        copies[-1].start()
    for copy in copies:
        copy.wait()


def statistics(logits, square, student, out_ref, rows):
    mean = jnp.sum(square, axis=1, keepdims=True) / (BLOCKS * 512)
    teach = logits * lax.rsqrt(mean + 1e-05)
    out_ref[rows, :] = teach
    stud = student.astype(jnp.float32)
    teach_peak = jnp.max(teach, axis=1, keepdims=True)
    stud_peak = jnp.max(stud, axis=1, keepdims=True)
    teach = teach - teach_peak
    stud = stud - stud_peak
    mass = jnp.exp(stud)
    teach_total = jnp.sum(jnp.exp(teach), axis=1, keepdims=True)
    stud_total = jnp.sum(mass, axis=1, keepdims=True)
    cross = jnp.sum(mass * (stud - teach), axis=1, keepdims=True)
    lane = lax.broadcasted_iota(jnp.int32, (CHUNK, 128), 1)
    packed = jnp.zeros((CHUNK, 128), jnp.float32)
    for at, value in enumerate((teach_peak, teach_total, stud_peak, stud_total, cross)):
        packed = jnp.where(lane == at, value, packed)
    return packed.T[:8, :]


def accumulate_blocks(gain, student, plan, first, blocks, near, far, state=None):
    tok, cols = student.shape
    hbm = pl.BlockSpec(memory_space=pltpu.HBM)
    vmem = pl.BlockSpec(memory_space=pltpu.VMEM)
    smem = pl.BlockSpec(memory_space=pltpu.SMEM)
    anywhere = pl.BlockSpec(memory_space=pl.ANY)
    logits = jax.ShapeDtypeStruct((tok, cols), jnp.float32)
    totals = jax.ShapeDtypeStruct((8 * tok, cols + 128), jnp.float32)
    stats = jax.ShapeDtypeStruct((8, tok), jnp.float32)
    count = len(blocks)
    last = first + count == BLOCKS
    scratch = [
        pltpu.VMEM((tok, cols + 128), jnp.float32),
        pltpu.VMEM((count, tok, 512), jnp.bfloat16),
        pltpu.VMEM((count, 512, cols), jnp.bfloat16),
        pltpu.SemaphoreType.DMA((count,)),
        pltpu.SemaphoreType.DMA((count,)),
        pltpu.SemaphoreType.DMA,
        pltpu.SemaphoreType.DMA((tok // CHUNK,)),
    ]
    if first:
        scratch += [pltpu.VMEM((tok, cols + 128), jnp.float32)]
    if last:
        scratch += [
            pltpu.VMEM((tok, cols), jnp.bfloat16),
            pltpu.SemaphoreType.DMA,
        ]
    parts = [student] * last + [state] * (first > 0) + [one for block in blocks for one in block]
    return pl.pallas_call(
        functools.partial(teacher_kernel, first, [len(block) for block in blocks]),
        out_shape=(logits, stats) if last else totals,
        in_specs=[smem, vmem] + [hbm] * 2 + [anywhere] * len(parts),
        out_specs=(vmem, vmem) if last else hbm,
        scratch_shapes=scratch,
        compiler_params=pltpu.CompilerParams(vmem_limit_bytes=(42 if last else 60) * MIB),
        name="teacher_" + str(first),
    )(plan, gain.reshape(BLOCKS, 1, 512), near, far, *parts)


def merge(first, second):
    teach_peak = jnp.maximum(first[0], second[0])
    stud_peak = jnp.maximum(first[2], second[2])
    teach_total = stud_total = cross = 0.0
    for part in (first, second):
        teach_low = part[0] - teach_peak
        stud_low = part[2] - stud_peak
        weight = jnp.exp(stud_low)
        teach_total = teach_total + jnp.exp(teach_low) * part[1]
        stud_total = stud_total + weight * part[3]
        cross = cross + weight * (part[4] + part[3] * (stud_low - teach_low))
    log_stud = jnp.log(stud_total)
    log_teach = jnp.log(teach_total)
    divergence = cross / stud_total - (log_stud - log_teach)
    offset = (stud_peak - teach_peak) + (log_stud - log_teach) + divergence
    return stud_peak, log_stud, offset, divergence


def combine_kernel(own_ref, near_ref, third_ref, fourth_ref, live_ref, count_ref, coef_ref, sums_ref):
    parts = [
        [ref[at : at + 1, :] for at in range(5)]
        for ref in (own_ref, near_ref, third_ref, fourth_ref)
    ]
    live = live_ref[...]
    stud_peak, log_stud, offset, divergence = merge(parts[0], parts[1])
    other_divergence = merge(parts[2], parts[3])[3]
    coef_ref[...] = jnp.zeros_like(coef_ref)
    coef_ref[0:1, :] = stud_peak
    coef_ref[1:2, :] = log_stud
    coef_ref[2:3, :] = offset
    coef_ref[3:4, :] = V * live
    lane = lax.broadcasted_iota(jnp.int32, (1, 128), 1)
    total = jnp.sum(live * (divergence + other_divergence), axis=1, keepdims=True)
    sums_ref[...] = jnp.where(lane == 0, total, jnp.where(lane == 1, count_ref[0], 0.0))


def combine(stats, others, live, count):
    vmem = pl.BlockSpec(memory_space=pltpu.VMEM)
    return pl.pallas_call(
        combine_kernel,
        out_shape=(
            jax.ShapeDtypeStruct(stats.shape, jnp.float32),
            jax.ShapeDtypeStruct((1, 128), jnp.float32),
        ),
        in_specs=[vmem] * 5 + [pl.BlockSpec(memory_space=pltpu.SMEM)],
        out_specs=(vmem, vmem),
        compiler_params=pltpu.CompilerParams(vmem_limit_bytes=4 * MIB),
        name="combine",
    )(stats, *others, live, count)


def grad_kernel(coef_ref, teach_ref, student_ref, grad_ref):
    coef = coef_ref[...].T
    stud = student_ref[...].astype(jnp.float32)
    prob = jnp.exp((stud - coef[:, 0:1]) - coef[:, 1:2])
    differ = (stud - teach_ref[...]) - coef[:, 2:3]
    grad_ref[...] = ((coef[:, 3:4] * prob) * differ).astype(jnp.bfloat16)


def gradient(coef, teach, student):
    tok, cols = student.shape
    tile = 384
    rows = pl.BlockSpec((tile, cols), lambda i: (i, 0))
    return pl.pallas_call(
        grad_kernel,
        grid=(tok // tile,),
        out_shape=jax.ShapeDtypeStruct((tok, cols), jnp.bfloat16),
        in_specs=[pl.BlockSpec((8, tile), lambda i: (0, i)), rows, rows],
        out_specs=rows,
        compiler_params=pltpu.CompilerParams(vmem_limit_bytes=24 * MIB),
        name="gradient",
    )(coef, teach, student)


def stage(value, axis, moves):
    return sum([lax.ppermute(value, axis, move) for move in moves], value)


def body(teacher_hidden, norm_gain, head_weight, student_logits, row_lengths):
    tok = teacher_hidden.shape[0]
    steps_of = jnp.arange(tok, dtype=jnp.int32) % STEPS
    live = (steps_of < jnp.repeat(row_lengths, STEPS)).astype(jnp.float32)
    count = jnp.sum(row_lengths.astype(jnp.float32))
    accumulate = functools.partial(accumulate_blocks, norm_gain, student_logits, block_plan())
    teach, stats = teacher_logits(head_weight, teacher_hidden, accumulate)
    others = [
        lax.ppermute(stats, "tp", [(t, t ^ m) for t in range(BLOCKS)]) for m in (1, 2, 3)
    ]
    coef, sums = combine(stats, others, live.reshape(1, tok), count.reshape(1))

    sums = stage(sums, "rows", [row_xor(1)])
    sums = stage(sums, "rows", [row_xor(8)])
    grad = gradient(coef, teach, student_logits)
    sums, grad = lax.optimization_barrier((sums, grad))
    sums = stage(sums, "rows", [y_ring(d) for d in (1, 2, 3)])
    sums = stage(sums, "tp", [x_ring(d) for d in (1, 2, 3)])
    loss = sums[0, 0] / (CB * (sums[0, 1] / NX))
    return (grad, loss)


def solution(mesh):
    in_specs = (P("rows", "tp"), P(), P("rows", "tp"), P("rows", "tp"), P("rows"))
    out_specs = (P("rows", "tp"), P())
    return jax.shard_map(body, mesh=mesh, in_specs=in_specs, out_specs=out_specs, check_vma=False)
```
